512 devices in a mesh: dp: 64 (over z, x, core), mp: 8 (over y).
Axes of the slice: x: 4, y: 8, z: 8, core: 2. Of those that a mesh axis runs over, the one named last changes fastest.
Arguments:
- activations: bfloat16 [8, 128, 64, 5120], P('mp', 'dp'), may hold values from -6 to 6
- out_grads: bfloat16 [8, 128, 64, 5120], P('mp', 'dp'), may hold values from -6 to 6
- proj_in: bfloat16 [8, 64, 5120], P('mp'), may hold values from -0.078125 to 0.078125
- proj_out: bfloat16 [8, 64, 5120], P('mp'), may hold values from -0.078125 to 0.078125
- query_feat: float32 [8, 1024, 4096], P('mp', 'dp'), may hold values from -6 to 6
- candidates: int32 [64, 8], P('dp'), may hold values from 0 to 63
Outputs:
- gram: float32 [8, 4096, 4096], P('mp', 'dp')
- influence: float32 [1024, 16], P('dp')
The draws below stay inside these ranges and needn't reach their ends.
Inputs may be any that keep to these rules, and one draw needn't show every extreme that they name: `candidates`: each entry names a training shard; duplicates may occur.
All inputs are finite; a program needn't handle non-finite values.
Results may differ from the reference program's by a relative error of at most 0.0089.
Values may be sent and summed in bfloat16 or wider, within the bound.
A program may use at most 64 MiB of HBM per device.

```python
import math
import jax
import jax.numpy as jnp
import numpy as np
from jax import lax

D = 5120
RANK = 64
FEAT = 4096
MODULES = 8
SEQ_DEV = 2
SEQS = 128
TOK_SEQ = 64
QRY_DEV = 16
QUERIES = 1024
CAND = 8
ITERS = 6
N_DP = 64


def touch_ends(entries, stream_key, least, top_value):
    index_at = [jax.random.randint(jax.random.fold_in(stream_key, axis), (), 0, length) for axis, length in enumerate(entries.shape)]
    main_axis = entries.shape.index(max(entries.shape))
    neighbour = index_at[:main_axis] + [(index_at[main_axis] + 1) % entries.shape[main_axis]] + index_at[main_axis + 1:]
    return entries.at[tuple(index_at)].set(least).at[tuple(neighbour)].set(top_value)


def level_of(stream_key, dims, pieces, least, largest):
    loudness, own = 1.0, jax.random.fold_in(stream_key, 6)
    for dim, blocks in pieces:
        steps = jnp.exp(jax.random.uniform(jax.random.fold_in(own, dim), (blocks,), jnp.float32, least / len(pieces), largest / len(pieces)))
        loudness = loudness * jnp.repeat(steps, dims[dim] // blocks).reshape([-1 if axis == dim else 1 for axis in range(len(dims))])
    return loudness


def rank_bounds(number_of, slope):
    loads = [(1 << 20) // math.isqrt(rank ** slope) + 1 for rank in range(1, number_of + 1)]
    width = 1 + sum(loads) // (1 << 30)
    return np.cumsum(np.array([max(1, weight // width) for weight in loads]))


def ranked(rng, extent, amount, skew):
    table = rank_bounds(amount, skew)
    pick = jax.random.randint(jax.random.fold_in(rng, 1), extent, 0, int(table[amount - 1]))
    standing = jnp.searchsorted(jnp.asarray(table, jnp.int32), pick, side="right")
    return jax.random.permutation(jax.random.fold_in(rng, 2), amount)[standing].astype(jnp.int32)


def normal_values(key, extent, scale, reach, split=(), kind=jnp.bfloat16):
    entries = jax.random.normal(key, extent, jnp.float32) * scale
    if len(split) > 0:
        entries = level_of(key, extent, split, -0.22, 0.18) * entries
    return jnp.clip(entries, min=-reach, max=reach).astype(kind)


def setup_inputs(seed: int = 0) -> dict:
    seeds = jax.random.split(jax.random.key(seed), 7)
    activations = normal_values(seeds[0], (MODULES, SEQS, TOK_SEQ, D), 1.0, 6.0, ((0, 8), (1, 64)))
    out_grads = normal_values(seeds[1], (MODULES, SEQS, TOK_SEQ, D), 1.0, 6.0, ((0, 8), (1, 64)))
    proj_in = normal_values(seeds[2], (MODULES, RANK, D), D ** -0.5, 0.078125, ((0, 8),))
    proj_out = normal_values(seeds[3], (MODULES, RANK, D), D ** -0.5, 0.078125, ((0, 8),))
    query_feat = normal_values(seeds[4], (MODULES, QUERIES, FEAT), 1.0, 6.0, ((0, 8), (1, 64)), jnp.float32)
    candidates = touch_ends(ranked(seeds[5], (N_DP, CAND), N_DP, 2), jax.random.fold_in(seeds[5], 3), 0, N_DP - 1).astype(jnp.int32)
    return {"activations": activations, "out_grads": out_grads, "proj_in": proj_in, "proj_out": proj_out, "query_feat": query_feat, "candidates": candidates}


def apply_op(features_all, damping, vectors):
    inner = jnp.einsum('msf,mqf->mqs', features_all, vectors, precision=lax.Precision.HIGHEST)
    back = jnp.einsum('msf,mqs->mqf', features_all, inner, precision=lax.Precision.HIGHEST)
    return back + damping[:, None, None] * vectors

def reference(activations, out_grads, proj_in, proj_out, query_feat, candidates):
    xin = jnp.einsum('mstd,mrd->mstr', activations.astype(jnp.float32), proj_in.astype(jnp.float32)).astype(jnp.bfloat16)
    gout = jnp.einsum('mstd,mrd->mstr', out_grads.astype(jnp.float32), proj_out.astype(jnp.float32)).astype(jnp.bfloat16)
    feats = jnp.einsum('msta,mstb->msab', gout.astype(jnp.float32), xin.astype(jnp.float32))
    feats = feats.reshape(MODULES, SEQS, FEAT)
    gram = jnp.einsum('msf,msg->mfg', feats, feats, precision=lax.Precision.HIGHEST)
    damping = 0.1 * lax.optimization_barrier(jnp.sum(feats * feats, axis=(1, 2))) / FEAT
    solution = jnp.zeros_like(query_feat)
    resid = query_feat
    direction = query_feat
    resid_sq = lax.optimization_barrier(jnp.sum(resid * resid, axis=2))
    for iteration in range(ITERS):
        image = apply_op(feats, damping, direction)
        alpha = resid_sq / lax.optimization_barrier(jnp.sum(direction * image, axis=2))
        solution = solution + alpha[:, :, None] * direction
        resid = resid - alpha[:, :, None] * image
        next_sq = lax.optimization_barrier(jnp.sum(resid * resid, axis=2))
        direction = resid + (next_sq / resid_sq)[:, :, None] * direction
        resid_sq = next_sq
    selfsum = lax.optimization_barrier(jnp.sum(solution * query_feat, axis=(0, 2)))
    shard_view = feats.reshape(MODULES, N_DP, SEQ_DEV, FEAT)
    blocked = solution.reshape(MODULES, N_DP, QRY_DEV, FEAT).transpose(1, 0, 2, 3)

    def block_scores(items):
        sol_block, cand_row = items
        chosen = shard_view[:, cand_row]
        scores = jnp.einsum('mqf,mcjf->qcj', sol_block, chosen, precision=lax.Precision.HIGHEST)
        return scores.reshape(QRY_DEV, CAND * SEQ_DEV)
    total = lax.map(block_scores, (blocked, candidates)).reshape(QUERIES, CAND * SEQ_DEV)
    influence = total / jnp.sqrt(selfsum)[:, None]
    return (gram, influence)
```

```python
import functools

import jax
import jax.numpy as jnp
from jax import lax
from jax.experimental import pallas as pl
from jax.experimental.pallas import tpu as pltpu
from jax.sharding import PartitionSpec as P

ITERS = 6
NZ, NX, NC = 8, 4, 2
GROUPS = NX * NC
CHUNKS = 4
MESH = pl.DeviceIdType.MESH
F32 = jnp.float32
BF16 = jnp.bfloat16
Z_ORDER = (1, 7, 2, 6, 3, 5, 4)


def dot_nt(lhs, rhs):
    return lax.dot_general(lhs, rhs, (((1,), (1,)), ((), ())), preferred_element_type=F32)


def dot_nn(lhs, rhs):
    return jnp.dot(lhs, rhs, preferred_element_type=F32)


def high_low(value):
    high = value.astype(BF16)
    return high, (value - high.astype(F32)).astype(BF16)


def kernel(
    cand_ref, act_hbm, grad_hbm, pin_hbm, pout_hbm, query_hbm,
    gram_hbm, infl_ref,
    act, grad, pin, pout, query, raw, wide, feats, turned, lhs_query, gram, parts,
    in_sem, query_sem, send_sem, z_sem, raw_sem, part_send, part_sem, gram_sem,
):
    dp = lax.axis_index("dp")
    mp = lax.axis_index("mp")
    modules = parts.shape[0]
    zi, group = dp // GROUPS, dp % GROUPS
    xi, core = group // NC, group % NC

    width = act.shape[1] // CHUNKS
    loads = []
    for chunk in range(CHUNKS):
        cols = pl.ds(chunk * width, width)
        row = []
        for which, (src, dst) in enumerate(((pout_hbm, pout), (grad_hbm, grad), (pin_hbm, pin), (act_hbm, act))):
            row.append(pltpu.make_async_copy(src.at[:, cols], dst.at[:, cols], in_sem.at[chunk, which]))
        loads.append(row)
        for copy in row:
            copy.start()
    query_load = pltpu.make_async_copy(query_hbm, query, query_sem)
    query_load.start()

    def dp_at(z, g):
        return {"dp": z * GROUPS + g}

    mate = dp_at(zi, xi * NC + (1 - core))
    z_peer = [(zi + step) % NZ for step in range(NZ)]
    x_peer = [((xi + step) % NX) * NC + core for step in range(NX)]
    m_peer = [(mp + step) % modules for step in range(modules)]

    barrier = pltpu.get_barrier_semaphore()
    for step in range(1, NZ):
        pl.semaphore_signal(barrier, 1, device_id=dp_at(z_peer[step], group), device_id_type=MESH)
    for step in range(1, NX):
        pl.semaphore_signal(barrier, 1, device_id=dp_at(zi, x_peer[step]), device_id_type=MESH)
    pl.semaphore_signal(barrier, 1, device_id=mate, device_id_type=MESH)
    for step in range(1, modules):
        pl.semaphore_signal(barrier, 1, device_id={"mp": m_peer[step]}, device_id_type=MESH)

    gout = jnp.zeros((pout.shape[0], grad.shape[0]), F32)
    xin = jnp.zeros((act.shape[0], 2 * pin.shape[0]), F32)
    for chunk in range(CHUNKS):
        cols = slice(chunk * width, (chunk + 1) * width)
        loads[chunk][0].wait()
        loads[chunk][1].wait()
        gout += dot_nt(pout[:, cols], grad[:, cols])
        loads[chunk][2].wait()
        loads[chunk][3].wait()
        pin_cols = pin[:, cols]
        xin += dot_nt(act[:, cols], jnp.concatenate([pin_cols, pin_cols], axis=0))

    rank = pout.shape[0]
    half = rank // 2
    turned[...] = gout
    stacked = jnp.concatenate(
        [turned[pl.ds(0, half, stride=2), :], turned[pl.ds(1, half, stride=2), :]], axis=0
    ).astype(BF16)
    token = lax.broadcasted_iota(jnp.int32, xin.shape, 0)
    tokens = act.shape[0] // 2
    both = jnp.concatenate(
        [jnp.where(token < tokens, xin, 0.0), jnp.where(token >= tokens, xin, 0.0)], axis=1
    ).astype(BF16)
    joined = dot_nn(stacked, both)
    lane = lax.broadcasted_iota(jnp.int32, (half, 2 * rank), 1)
    own = [
        jnp.where(lane < rank, joined[:half, s * 2 * rank:(s + 1) * 2 * rank], joined[half:, s * 2 * rank:(s + 1) * 2 * rank])
        for s in range(2)
    ]
    raw[group * NZ + zi] = jnp.concatenate(own, axis=0).astype(BF16)

    pl.semaphore_wait(barrier, (NZ - 1) + (NX - 1) + 1 + (modules - 1))

    def move(g, z, target, arrival):
        return pltpu.make_async_remote_copy(
            src_ref=raw.at[g * NZ + z], dst_ref=raw.at[g * NZ + z], send_sem=send_sem, recv_sem=arrival,
            device_id=target, device_id_type=MESH,
        )

    def spread(z):
        for step in range(1, NX):
            move(group, z, dp_at(zi, x_peer[step]), raw_sem.at[group, z]).start()
        move(group, z, mate, raw_sem.at[group, z]).start()

    def relay(z):
        for step in range(1, NX):
            g = x_peer[step]
            move(g, z, mate, raw_sem.at[g, z]).wait_recv()
            move(g, z, mate, raw_sem.at[g, z]).start()

    for step in Z_ORDER:
        move(group, zi, dp_at(z_peer[step], group), z_sem.at[zi]).start()
    spread(zi)
    query_load.wait()
    query_high, query_low = high_low(query[...])
    lhs_query[:16, :] = query_high
    lhs_query[16:, :] = query_low
    query_sq = jnp.sum(query[...] * query[...], axis=1, keepdims=True)

    before = zi
    for step in Z_ORDER:
        z = (zi - step + NZ) % NZ
        move(group, z, mate, z_sem.at[z]).wait_recv()
        spread(z)
        relay(before)
        before = z
    relay(before)
    for step in range(NX):
        g = ((xi + step) % NX) * NC + (1 - core)
        for z in range(NZ):
            move(g, z, mate, raw_sem.at[g, z]).wait_recv()

    rows = half
    seqs = GROUPS * NZ * 2
    wide[...] = raw[...].reshape(seqs * rows, 2 * rank).astype(F32)
    for r in range(rows):
        feats[:, r * 128:(r + 1) * 128] = wide[pl.ds(r, seqs, stride=rows), :].astype(BF16)
    tile = feats[...]
    inner = dot_nt(jnp.concatenate([tile, lhs_query[...]], axis=0), tile)
    kmat = inner[:seqs]
    u = inner[seqs:seqs + 16] + inner[seqs + 16:]
    eye = lax.broadcasted_iota(jnp.int32, (seqs, seqs), 0) == lax.broadcasted_iota(jnp.int32, (seqs, seqs), 1)
    trace = jnp.sum(jnp.sum(jnp.where(eye, kmat, 0.0), axis=1, keepdims=True), axis=0, keepdims=True)
    damping = 0.1 * trace / (rows * 2 * rank)
    k_high, k_low = high_low(kmat)
    k_both = jnp.concatenate([k_high, k_low], axis=1)

    def apply_k(v):
        v_high, v_low = high_low(v)
        out = dot_nn(jnp.concatenate([v_high, v_low], axis=0), k_both)
        return out[:16, :seqs] + (out[:16, seqs:] + out[16:, :seqs])

    w, v = u, u
    y = jnp.zeros_like(u)
    y_dir = jnp.zeros_like(u)
    c = jnp.ones_like(query_sq)
    c_dir = jnp.ones_like(query_sq)
    resid_sq, dir_sq = query_sq, query_sq
    scores = jnp.zeros_like(u)
    selfterm = jnp.zeros_like(query_sq)
    for iteration in range(ITERS):
        alpha = resid_sq / (jnp.sum(v * v, axis=1, keepdims=True) + damping * dir_sq)
        scores = scores + alpha * v
        selfterm = selfterm + alpha * resid_sq
        if iteration == ITERS - 1:
            break
        image = apply_k(v) + damping * v
        w = w - alpha * image
        y = y - alpha * (v + damping * y_dir)
        c = c - alpha * damping * c_dir
        next_sq = c * c * query_sq + jnp.sum(y * (c * u + w), axis=1, keepdims=True)
        beta = next_sq / resid_sq
        v = w + beta * v
        y_dir = y + beta * y_dir
        c_dir = c + beta * c_dir
        dir_sq = next_sq + beta * beta * dir_sq
        resid_sq = next_sq

    col = lax.broadcasted_iota(jnp.int32, (seqs, 128), 1)
    spot = jnp.full((seqs, 128), -1, jnp.int32)
    cands = cand_ref.shape[1]
    for i in range(cands):
        shard = cand_ref[0, i]
        first = (shard % GROUPS) * (2 * NZ) + (shard // GROUPS) * 2
        spot = jnp.where(col // 2 == i, first + col % 2, spot)
    pick = jnp.where(lax.broadcasted_iota(jnp.int32, (seqs, 128), 0) == spot, 1.0, 0.0).astype(BF16)
    s_high, s_low = high_low(scores)
    s_last = (scores - s_high.astype(F32) - s_low.astype(F32)).astype(BF16)
    picked = dot_nn(jnp.concatenate([s_high, s_low, s_last], axis=0), pick)
    picked = picked[:16] + picked[16:32] + picked[32:]
    part_col = lax.broadcasted_iota(jnp.int32, (16, 128), 1)
    parts[mp] = jnp.where(part_col == 2 * cands, selfterm, picked)
    for step in range(1, modules):
        pltpu.make_async_remote_copy(
            src_ref=parts.at[mp], dst_ref=parts.at[mp], send_sem=part_send, recv_sem=part_sem.at[mp],
            device_id={"mp": m_peer[step]}, device_id_type=MESH,
        ).start()

    own_tile = feats[:, pl.ds(pl.multiple_of((dp // 2) * 128, 128), 128)].astype(F32).T
    own_rows = jnp.where(dp % 2 == 0, own_tile[:rank], own_tile[rank:]).astype(BF16)
    gram_chunks = 4
    gram_width = gram.shape[1] // gram_chunks
    stores = []
    for chunk in range(gram_chunks):
        cols = slice(chunk * gram_width, (chunk + 1) * gram_width)
        gram[:, cols] = dot_nn(own_rows, feats[:, cols])
        at = pl.ds(chunk * gram_width, gram_width)
        stores.append(pltpu.make_async_copy(gram.at[:, at], gram_hbm.at[:, at], gram_sem.at[chunk]))
        stores[-1].start()

    for step in range(1, modules):
        other = m_peer[step]
        pltpu.make_async_remote_copy(
            src_ref=parts.at[other], dst_ref=parts.at[other], send_sem=part_send, recv_sem=part_sem.at[other],
            device_id={"mp": other}, device_id_type=MESH,
        ).wait_recv()
    total = parts[0]
    for m in range(1, modules):
        total = total + parts[m]
    infl_ref[...] = total[:, :2 * cands] / jnp.sqrt(total[:, 2 * cands:2 * cands + 1])

    def all_sent(ref, count, sem):
        pltpu.make_async_remote_copy(
            src_ref=ref.at[pl.ds(0, count)], dst_ref=ref.at[pl.ds(0, count)], send_sem=sem, recv_sem=z_sem.at[0],
            device_id=mate, device_id_type=MESH,
        ).wait_send()

    all_sent(raw, NX * NZ + NZ * (NX - 1) + NZ - 1, send_sem)
    all_sent(parts, modules - 1, part_send)
    for copy in stores:
        copy.wait()


def on_device(activations, out_grads, proj_in, proj_out, query_feat, candidates):
    _, seqs, tokens, depth = activations.shape
    rank = proj_in.shape[1]
    queries, size = query_feat.shape[1:]
    modules = lax.axis_size("mp")
    shards = lax.axis_size("dp")
    total = shards * seqs
    vmem = pltpu.VMEM
    dma = pltpu.SemaphoreType.DMA
    gram, influence = pl.pallas_call(
        kernel,
        name="influence",
        out_shape=(
            jax.ShapeDtypeStruct((size // shards, size), F32),
            jax.ShapeDtypeStruct((queries, candidates.shape[1] * seqs), F32),
        ),
        in_specs=[pl.BlockSpec(memory_space=pltpu.SMEM)] + [pl.BlockSpec(memory_space=pl.ANY)] * 5,
        out_specs=(pl.BlockSpec(memory_space=pl.ANY), pl.BlockSpec(memory_space=pltpu.VMEM)),
        scratch_shapes=[
            vmem((seqs * tokens, depth), BF16),
            vmem((seqs * tokens, depth), BF16),
            vmem((rank, depth), BF16),
            vmem((rank, depth), BF16),
            vmem((queries, size), F32),
            vmem((GROUPS * NZ, seqs * size // 128, 128), BF16),
            vmem((total * size // 128, 128), F32),
            vmem((total, size), BF16),
            vmem((rank, seqs * tokens), F32),
            vmem((2 * queries, size), BF16),
            vmem((size // shards, size), F32),
            vmem((modules, queries, 128), F32),
            dma((CHUNKS, 4)),
            dma,
            dma,
            dma((NZ,)),
            dma((GROUPS, NZ)),
            dma,
            dma((modules,)),
            dma((4,)),
        ],
        compiler_params=pltpu.CompilerParams(
            collective_id=0, has_side_effects=True, vmem_limit_bytes=48 * 2**20
        ),
    )(
        candidates,
        activations.reshape(seqs * tokens, depth),
        out_grads.reshape(seqs * tokens, depth),
        proj_in.reshape(rank, depth),
        proj_out.reshape(rank, depth),
        query_feat.reshape(queries, size),
    )
    return gram[None], influence


def solution(mesh):
    placed = (
        P("mp", "dp", None, None),
        P("mp", "dp", None, None),
        P("mp", None, None),
        P("mp", None, None),
        P("mp", "dp", None),
        P("dp", None),
    )
    return jax.shard_map(
        on_device,
        mesh=mesh,
        in_specs=placed,
        out_specs=(P("mp", "dp", None), P("dp", None)),
        check_vma=False,
    )
```

```python
import functools

import jax
import jax.numpy as jnp
from jax import lax
from jax.experimental import pallas as pl
from jax.experimental.pallas import tpu as pltpu
from jax.sharding import PartitionSpec as P

ITERS = 6
NZ, NX, NC = 8, 4, 2
GROUPS = NX * NC
CHUNKS = 4
MESH = pl.DeviceIdType.MESH
F32 = jnp.float32
BF16 = jnp.bfloat16
X_ORDER = (1, 3, 2)
SLOTS = (0, 1, 7, 2, 6, 3, 5, 4)
DIRECT = (1, 7)
WAVES = ((2, 6), (3, 5, 4))


def dot_nt(lhs, rhs):
    return lax.dot_general(lhs, rhs, (((1,), (1,)), ((), ())), preferred_element_type=F32)


def dot_nn(lhs, rhs):
    return jnp.dot(lhs, rhs, preferred_element_type=F32)


def high_low(value):
    high = value.astype(BF16)
    return high, (value - high.astype(F32)).astype(BF16)


def kernel(
    cand_hbm, act_hbm, grad_hbm, pin_hbm, pout_hbm, query_hbm,
    gram_ref, infl_ref,
    cand, act, grad, pin, pout, query, raw, wide, feats, turned, lhs_query, parts,
    in_sem, query_sem, cand_sem, send_sem, block_sem, wave_sem, relay_sem, part_send, part_sem,
):
    dp = lax.axis_index("dp")
    mp = lax.axis_index("mp")
    modules = parts.shape[0]
    zi, group = dp // GROUPS, dp % GROUPS
    xi, core = group // NC, group % NC

    width = act.shape[1] // CHUNKS
    loads = []
    for chunk in range(CHUNKS):
        cols = pl.ds(chunk * width, width)
        row = []
        for which, (src, dst) in enumerate(((pout_hbm, pout), (grad_hbm, grad), (pin_hbm, pin), (act_hbm, act))):
            row.append(pltpu.make_async_copy(src.at[:, cols], dst.at[:, cols], in_sem.at[chunk, which]))
        loads.append(row)
        for copy in row:
            copy.start()
    query_load = pltpu.make_async_copy(query_hbm, query, query_sem)
    query_load.start()
    cand_load = pltpu.make_async_copy(cand_hbm, cand, cand_sem)
    cand_load.start()

    def dp_at(z, g):
        return {"dp": z * GROUPS + g}

    mate = dp_at(zi, xi * NC + (1 - core))
    z_peer = [(zi + step) % NZ for step in range(NZ)]
    x_peer = [((xi + step) % NX) * NC + core for step in range(NX)]
    m_peer = [(mp + step) % modules for step in range(modules)]

    barrier = pltpu.get_barrier_semaphore()
    for step in range(1, NZ):
        pl.semaphore_signal(barrier, 1, device_id=dp_at(z_peer[step], group), device_id_type=MESH)
    for step in range(1, NX):
        pl.semaphore_signal(barrier, 1, device_id=dp_at(zi, x_peer[step]), device_id_type=MESH)
    for distance in DIRECT:
        for step in range(1, NX):
            pl.semaphore_signal(barrier, 1, device_id=dp_at(z_peer[distance], x_peer[step]), device_id_type=MESH)
    pl.semaphore_signal(barrier, 1, device_id=mate, device_id_type=MESH)
    for step in range(1, modules):
        pl.semaphore_signal(barrier, 1, device_id={"mp": m_peer[step]}, device_id_type=MESH)

    gout = jnp.zeros((pout.shape[0], grad.shape[0]), F32)
    xin = jnp.zeros((act.shape[0], 2 * pin.shape[0]), F32)
    for chunk in range(CHUNKS):
        cols = slice(chunk * width, (chunk + 1) * width)
        loads[chunk][0].wait()
        loads[chunk][1].wait()
        gout += dot_nt(pout[:, cols], grad[:, cols])
        loads[chunk][2].wait()
        loads[chunk][3].wait()
        pin_cols = pin[:, cols]
        xin += dot_nt(act[:, cols], jnp.concatenate([pin_cols, pin_cols], axis=0))

    rank = pout.shape[0]
    half = rank // 2
    turned[...] = gout
    stacked = jnp.concatenate(
        [turned[pl.ds(0, half, stride=2), :], turned[pl.ds(1, half, stride=2), :]], axis=0
    ).astype(BF16)
    token = lax.broadcasted_iota(jnp.int32, xin.shape, 0)
    tokens = act.shape[0] // 2
    both = jnp.concatenate(
        [jnp.where(token < tokens, xin, 0.0), jnp.where(token >= tokens, xin, 0.0)], axis=1
    ).astype(BF16)
    joined = dot_nn(stacked, both)
    lane = lax.broadcasted_iota(jnp.int32, (half, 2 * rank), 1)
    own = [
        jnp.where(lane < rank, joined[:half, s * 2 * rank:(s + 1) * 2 * rank], joined[half:, s * 2 * rank:(s + 1) * 2 * rank])
        for s in range(2)
    ]
    raw[group * NZ] = jnp.concatenate(own, axis=0).astype(BF16)

    pl.semaphore_wait(barrier, (NZ - 1) + (1 + len(DIRECT)) * (NX - 1) + 1 + (modules - 1))

    def remote(src, dst, target, arrival):
        return pltpu.make_async_remote_copy(
            src_ref=src, dst_ref=dst, send_sem=send_sem, recv_sem=arrival, device_id=target, device_id_type=MESH
        )

    def blocks(g, first, count):
        return raw.at[pl.ds(g * NZ + first, count)]

    def send_own(distance, step):
        slot = SLOTS.index(distance)
        target = dp_at(z_peer[(NZ - distance) % NZ], x_peer[step])
        remote(blocks(group, 0, 1), blocks(group, slot, 1), target, block_sem.at[group, slot]).start()

    def wait_block(g, slot):
        remote(blocks(g, slot, 1), blocks(g, slot, 1), mate, block_sem.at[g, slot]).wait_recv()

    def wave(g, number, target):
        slots = [SLOTS.index(distance) for distance in WAVES[number]]
        at = blocks(g, slots[0], len(slots))
        return remote(at, at, target, wave_sem.at[g, number])

    def relay(g):
        return remote(blocks(g, 0, NZ), blocks(g, 0, NZ), mate, relay_sem.at[g])

    for step in X_ORDER:
        send_own(0, step)
    for distance in (4, 3, 5, 2, 6, 1, 7):
        send_own(distance, 0)
    for distance in DIRECT:
        for step in X_ORDER:
            send_own(distance, step)
    query_load.wait()
    cand_load.wait()
    query_high, query_low = high_low(query[...])
    lhs_query[:16, :] = query_high
    lhs_query[16:, :] = query_low
    query_sq = jnp.sum(query[...] * query[...], axis=1, keepdims=True)

    rows = half
    seqs = GROUPS * NZ * 2
    group_rows = NZ * 2 * rows
    group_seqs = NZ * 2

    def lay_out(place, g):
        base = place * group_rows
        wide[base:base + group_rows] = raw[pl.ds(g * NZ, NZ)].reshape(group_rows, 2 * rank).astype(F32)
        at = pl.ds(pl.multiple_of(g * group_seqs, group_seqs), group_seqs)
        for r in range(rows):
            feats[at, r * 128:(r + 1) * 128] = wide[pl.ds(base + r, group_seqs, stride=rows), :].astype(BF16)

    for number in range(len(WAVES)):
        for distance in WAVES[number]:
            wait_block(group, SLOTS.index(distance))
        for step in X_ORDER:
            wave(group, number, dp_at(zi, x_peer[step])).start()
    for distance in DIRECT:
        wait_block(group, SLOTS.index(distance))
    relay(group).start()
    lay_out(0, group)
    for place, step in enumerate(X_ORDER):
        g = x_peer[step]
        wait_block(g, 0)
        for distance in DIRECT:
            wait_block(g, SLOTS.index(distance))
        for number in range(len(WAVES)):
            wave(g, number, mate).wait_recv()
        relay(g).start()
        lay_out(1 + place, g)
    for place, step in enumerate((0,) + X_ORDER):
        g = ((xi + step) % NX) * NC + (1 - core)
        relay(g).wait_recv()
        lay_out(NX + place, g)

    tile = feats[...]
    inner = dot_nt(jnp.concatenate([tile, lhs_query[...]], axis=0), tile)
    kmat = inner[:seqs]
    u = inner[seqs:seqs + 16] + inner[seqs + 16:]
    eye = lax.broadcasted_iota(jnp.int32, (seqs, seqs), 0) == lax.broadcasted_iota(jnp.int32, (seqs, seqs), 1)
    trace = jnp.sum(jnp.sum(jnp.where(eye, kmat, 0.0), axis=1, keepdims=True), axis=0, keepdims=True)
    damping = 0.1 * trace / (rows * 2 * rank)
    k_high, k_low = high_low(kmat)
    k_both = jnp.concatenate([k_high, k_low], axis=1)

    def apply_k(v):
        v_high, v_low = high_low(v)
        out = dot_nn(jnp.concatenate([v_high, v_low], axis=0), k_both)
        return out[:16, :seqs] + (out[:16, seqs:] + out[16:, :seqs])

    w, v = u, u
    y = jnp.zeros_like(u)
    y_dir = jnp.zeros_like(u)
    c = jnp.ones_like(query_sq)
    c_dir = jnp.ones_like(query_sq)
    resid_sq, dir_sq = query_sq, query_sq
    scores = jnp.zeros_like(u)
    selfterm = jnp.zeros_like(query_sq)
    for iteration in range(ITERS):
        alpha = resid_sq / (jnp.sum(v * v, axis=1, keepdims=True) + damping * dir_sq)
        scores = scores + alpha * v
        selfterm = selfterm + alpha * resid_sq
        if iteration == ITERS - 1:
            break
        image = apply_k(v) + damping * v
        w = w - alpha * image
        y = y - alpha * (v + damping * y_dir)
        c = c - alpha * damping * c_dir
        next_sq = c * c * query_sq + jnp.sum(y * (c * u + w), axis=1, keepdims=True)
        beta = next_sq / resid_sq
        v = w + beta * v
        y_dir = y + beta * y_dir
        c_dir = c + beta * c_dir
        dir_sq = next_sq + beta * beta * dir_sq
        resid_sq = next_sq

    col = lax.broadcasted_iota(jnp.int32, (seqs, 128), 1)
    spot = jnp.full((seqs, 128), -1, jnp.int32)
    cands = cand.shape[1]
    for i in range(cands):
        shard = cand[0, i]
        distance = (shard // GROUPS + NZ - zi) % NZ
        slot = jnp.where(distance == 0, 0, jnp.where(distance <= NZ // 2, 2 * distance - 1, 2 * (NZ - distance)))
        first = (shard % GROUPS) * group_seqs + slot * 2
        spot = jnp.where(col // 2 == i, first + col % 2, spot)
    pick = jnp.where(lax.broadcasted_iota(jnp.int32, (seqs, 128), 0) == spot, 1.0, 0.0).astype(BF16)
    s_high, s_low = high_low(scores)
    s_last = (scores - s_high.astype(F32) - s_low.astype(F32)).astype(BF16)
    picked = dot_nn(jnp.concatenate([s_high, s_low, s_last], axis=0), pick)
    picked = picked[:16] + picked[16:32] + picked[32:]
    part_col = lax.broadcasted_iota(jnp.int32, (16, 128), 1)
    parts[mp] = jnp.where(part_col == 2 * cands, selfterm, picked)
    for step in range(1, modules):
        pltpu.make_async_remote_copy(
            src_ref=parts.at[mp], dst_ref=parts.at[mp], send_sem=part_send, recv_sem=part_sem.at[mp],
            device_id={"mp": m_peer[step]}, device_id_type=MESH,
        ).start()

    own_tile = feats[:, pl.ds(pl.multiple_of((dp // 2) * 128, 128), 128)].astype(F32).T
    own_rows = jnp.where(dp % 2 == 0, own_tile[:rank], own_tile[rank:]).astype(BF16)
    gram_chunks = 4
    gram_width = gram_ref.shape[1] // gram_chunks
    for chunk in range(gram_chunks):
        cols = slice(chunk * gram_width, (chunk + 1) * gram_width)
        gram_ref[:, cols] = dot_nn(own_rows, feats[:, cols])

    for step in range(1, modules):
        other = m_peer[step]
        pltpu.make_async_remote_copy(
            src_ref=parts.at[other], dst_ref=parts.at[other], send_sem=part_send, recv_sem=part_sem.at[other],
            device_id={"mp": other}, device_id_type=MESH,
        ).wait_recv()
    total = parts[0]
    for m in range(1, modules):
        total = total + parts[m]
    infl_ref[...] = total[:, :2 * cands] / jnp.sqrt(total[:, 2 * cands:2 * cands + 1])

    def all_sent(ref, count, sem):
        pltpu.make_async_remote_copy(
            src_ref=ref.at[pl.ds(0, count)], dst_ref=ref.at[pl.ds(0, count)], send_sem=sem, recv_sem=relay_sem.at[0],
            device_id=mate, device_id_type=MESH,
        ).wait_send()

    own_copies = (NX - 1) + (NZ - 1) + len(DIRECT) * (NX - 1)
    wave_copies = sum(len(distances) for distances in WAVES) * (NX - 1)
    all_sent(raw, own_copies + wave_copies + NX * NZ, send_sem)
    all_sent(parts, modules - 1, part_send)


def write_kernel(gram_ref, infl_ref, gram_out, infl_out, gram_sem, infl_sem):
    gram_copy = pltpu.make_async_copy(gram_ref, gram_out, gram_sem)
    infl_copy = pltpu.make_async_copy(infl_ref, infl_out, infl_sem)
    gram_copy.start()
    infl_copy.start()
    infl_copy.wait()
    gram_copy.wait()


def on_device(activations, out_grads, proj_in, proj_out, query_feat, candidates):
    _, seqs, tokens, depth = activations.shape
    rank = proj_in.shape[1]
    queries, size = query_feat.shape[1:]
    modules = lax.axis_size("mp")
    shards = lax.axis_size("dp")
    total = shards * seqs
    vmem = pltpu.VMEM
    dma = pltpu.SemaphoreType.DMA
    gram, influence = pl.pallas_call(
        kernel,
        name="influence",
        out_shape=(
            jax.ShapeDtypeStruct((size // shards, size), F32),
            jax.ShapeDtypeStruct((queries, candidates.shape[1] * seqs), F32),
        ),
        in_specs=[pl.BlockSpec(memory_space=pltpu.HBM)] * 6,
        out_specs=(pl.BlockSpec(memory_space=pltpu.VMEM), pl.BlockSpec(memory_space=pltpu.VMEM)),
        scratch_shapes=[
            pltpu.SMEM(candidates.shape, jnp.int32),
            vmem((seqs * tokens, depth), BF16),
            vmem((seqs * tokens, depth), BF16),
            vmem((rank, depth), BF16),
            vmem((rank, depth), BF16),
            vmem((queries, size), F32),
            vmem((GROUPS * NZ, seqs * size // 128, 128), BF16),
            vmem((total * size // 128, 128), F32),
            vmem((total, size), BF16),
            vmem((rank, seqs * tokens), F32),
            vmem((2 * queries, size), BF16),
            vmem((modules, queries, 128), F32),
            dma((CHUNKS, 4)),
            dma,
            dma,
            dma,
            dma((GROUPS, NZ)),
            dma((GROUPS, len(WAVES))),
            dma((GROUPS,)),
            dma,
            dma((modules,)),
        ],
        compiler_params=pltpu.CompilerParams(
            collective_id=0, has_side_effects=True, vmem_limit_bytes=48 * 2**20
        ),
    )(
        *(
            pltpu.with_memory_space_constraint(operand, pltpu.HBM)
            for operand in (
                candidates,
                activations.reshape(seqs * tokens, depth),
                out_grads.reshape(seqs * tokens, depth),
                proj_in.reshape(rank, depth),
                proj_out.reshape(rank, depth),
                query_feat.reshape(queries, size),
            )
        ),
    )
    gram, influence = pl.pallas_call(
        write_kernel,
        name="write",
        out_shape=(jax.ShapeDtypeStruct(gram.shape, F32), jax.ShapeDtypeStruct(influence.shape, F32)),
        in_specs=[pl.BlockSpec(memory_space=pltpu.VMEM)] * 2,
        out_specs=[pl.BlockSpec(memory_space=pltpu.HBM)] * 2,
        scratch_shapes=[dma, dma],
        compiler_params=pltpu.CompilerParams(vmem_limit_bytes=2**20),
    )(gram, influence)
    return gram[None], influence


def solution(mesh):
    placed = (
        P("mp", "dp", None, None),
        P("mp", "dp", None, None),
        P("mp", None, None),
        P("mp", None, None),
        P("mp", "dp", None),
        P("dp", None),
    )
    return jax.shard_map(
        on_device,
        mesh=mesh,
        in_specs=placed,
        out_specs=(P("mp", "dp", None), P("dp", None)),
        check_vma=False,
    )
```

```python
import functools

import jax
import jax.numpy as jnp
from jax import lax
from jax.experimental import pallas as pl
from jax.experimental.pallas import tpu as pltpu
from jax.sharding import PartitionSpec as P

ITERS = 6
NZ, NX, NC = 8, 4, 2
GROUPS = NX * NC
CHUNKS = 4
MESH = pl.DeviceIdType.MESH
F32 = jnp.float32
BF16 = jnp.bfloat16
X_ORDER = (2, 1, 3)
SLOTS = (0, 1, 7, 2, 6, 3, 5, 4)
NEAR = (1, 7)
WAVES = ((2, 6, 3, 5, 4),)


def dot_nt(lhs, rhs):
    return lax.dot_general(lhs, rhs, (((1,), (1,)), ((), ())), preferred_element_type=F32)


def dot_nn(lhs, rhs):
    return jnp.dot(lhs, rhs, preferred_element_type=F32)


def high_low(value):
    high = value.astype(BF16)
    return high, (value - high.astype(F32)).astype(BF16)


def kernel(
    cand_hbm, act_hbm, grad_hbm, pin_hbm, pout_hbm, query_hbm,
    gram_ref, infl_ref,
    cand, act, grad, pin, pout, query, raw, wide, feats, turned, lhs_query, pick, parts,
    in_sem, query_sem, cand_sem, send_sem, relay_send, block_sem, wave_sem, relay_sem, part_send, part_sem,
):
    dp = lax.axis_index("dp")
    mp = lax.axis_index("mp")
    modules = parts.shape[0]
    zi, group = dp // GROUPS, dp % GROUPS
    xi, core = group // NC, group % NC

    width = act.shape[1] // CHUNKS
    loads = []
    for chunk in range(CHUNKS):
        cols = pl.ds(chunk * width, width)
        row = []
        for which, (src, dst) in enumerate(((pout_hbm, pout), (grad_hbm, grad), (pin_hbm, pin), (act_hbm, act))):
            row.append(pltpu.make_async_copy(src.at[:, cols], dst.at[:, cols], in_sem.at[chunk, which]))
        loads.append(row)
        for copy in row:
            copy.start()
    query_load = pltpu.make_async_copy(query_hbm, query, query_sem)
    query_load.start()
    cand_load = pltpu.make_async_copy(cand_hbm, cand, cand_sem)
    cand_load.start()

    def dp_at(z, g):
        return {"dp": z * GROUPS + g}

    mate = dp_at(zi, xi * NC + (1 - core))
    z_peer = [(zi + step) % NZ for step in range(NZ)]
    x_peer = [((xi + step) % NX) * NC + core for step in range(NX)]
    m_peer = [(mp + step) % modules for step in range(modules)]

    barrier = pltpu.get_barrier_semaphore()
    for step in range(1, NZ):
        pl.semaphore_signal(barrier, 1, device_id=dp_at(z_peer[step], group), device_id_type=MESH)
    for step in range(1, NX):
        pl.semaphore_signal(barrier, 1, device_id=dp_at(zi, x_peer[step]), device_id_type=MESH)
    pl.semaphore_signal(barrier, 1, device_id=mate, device_id_type=MESH)
    for step in range(1, modules):
        pl.semaphore_signal(barrier, 1, device_id={"mp": m_peer[step]}, device_id_type=MESH)

    gout = jnp.zeros((pout.shape[0], grad.shape[0]), F32)
    xin = jnp.zeros((act.shape[0], 2 * pin.shape[0]), F32)
    for chunk in range(CHUNKS):
        cols = slice(chunk * width, (chunk + 1) * width)
        loads[chunk][0].wait()
        loads[chunk][1].wait()
        gout += dot_nt(pout[:, cols], grad[:, cols])
        loads[chunk][2].wait()
        loads[chunk][3].wait()
        pin_cols = pin[:, cols]
        xin += dot_nt(act[:, cols], jnp.concatenate([pin_cols, pin_cols], axis=0))

    rank = pout.shape[0]
    half = rank // 2
    turned[...] = gout
    stacked = jnp.concatenate(
        [turned[pl.ds(0, half, stride=2), :], turned[pl.ds(1, half, stride=2), :]], axis=0
    ).astype(BF16)
    token = lax.broadcasted_iota(jnp.int32, xin.shape, 0)
    tokens = act.shape[0] // 2
    both = jnp.concatenate(
        [jnp.where(token < tokens, xin, 0.0), jnp.where(token >= tokens, xin, 0.0)], axis=1
    ).astype(BF16)
    joined = dot_nn(stacked, both)
    lane = lax.broadcasted_iota(jnp.int32, (half, 2 * rank), 1)
    own = [
        jnp.where(lane < rank, joined[:half, s * 2 * rank:(s + 1) * 2 * rank], joined[half:, s * 2 * rank:(s + 1) * 2 * rank])
        for s in range(2)
    ]
    raw[xi * NZ] = jnp.concatenate(own, axis=0).astype(BF16)

    pl.semaphore_wait(barrier, (NZ - 1) + (NX - 1) + 1 + (modules - 1))

    rows = half
    seqs = GROUPS * NZ * 2
    group_rows = NZ * 2 * rows
    group_seqs = NZ * 2

    def seqs_of(x, other):
        return pl.ds(pl.multiple_of(other * (seqs // 2) + x * group_seqs, group_seqs), group_seqs)

    def lay_out(place, x):
        base = place * group_rows
        wide[base:base + group_rows] = raw[pl.ds(x * NZ, NZ)].reshape(group_rows, 2 * rank).astype(F32)
        for r in range(rows):
            feats[seqs_of(x, 0), r * 128:(r + 1) * 128] = wide[pl.ds(base + r, group_seqs, stride=rows), :].astype(BF16)

    def remote(src, dst, target, arrival):
        return pltpu.make_async_remote_copy(
            src_ref=src, dst_ref=dst, send_sem=send_sem, recv_sem=arrival, device_id=target, device_id_type=MESH
        )

    def blocks(x, first, count):
        return raw.at[pl.ds(x * NZ + first, count)]

    def send_own(distance, step):
        slot = SLOTS.index(distance)
        target = dp_at(z_peer[(NZ - distance) % NZ], x_peer[step])
        remote(blocks(xi, 0, 1), blocks(xi, slot, 1), target, block_sem.at[xi, slot]).start()

    def wait_block(x, slot):
        remote(blocks(x, slot, 1), blocks(x, slot, 1), mate, block_sem.at[x, slot]).wait_recv()

    def wave(x, number, target):
        slots = [SLOTS.index(distance) for distance in WAVES[number]]
        at = blocks(x, slots[0], len(slots))
        return remote(at, at, target, wave_sem.at[x, number])

    def relay(x):
        return pltpu.make_async_remote_copy(
            src_ref=feats.at[seqs_of(x, 0)], dst_ref=feats.at[seqs_of(x, 1)], send_sem=relay_send,
            recv_sem=relay_sem.at[x], device_id=mate, device_id_type=MESH,
        )

    for step in X_ORDER:
        send_own(0, step)
    for distance in (4, 3, 5, 2, 6, 1, 7):
        send_own(distance, 0)
    query_load.wait()
    cand_load.wait()
    query_high, query_low = high_low(query[...])
    lhs_query[:16, :] = query_high
    lhs_query[16:, :] = query_low
    query_sq = jnp.sum(query[...] * query[...], axis=1, keepdims=True)

    col = lax.broadcasted_iota(jnp.int32, (seqs, 128), 1)
    spot = jnp.full((seqs, 128), -1, jnp.int32)
    cands = cand.shape[1]
    for i in range(cands):
        shard = cand[0, i]
        distance = (shard // GROUPS + NZ - zi) % NZ
        slot = 0
        for number in range(1, NZ):
            slot = jnp.where(distance == SLOTS[number], number, slot)
        place = shard % GROUPS
        first = (place % NC + NC - core) % NC * (seqs // 2) + place // NC * group_seqs + slot * 2
        spot = jnp.where(col // 2 == i, first + col % 2, spot)
    pick[...] = jnp.where(lax.broadcasted_iota(jnp.int32, (seqs, 128), 0) == spot, 1.0, 0.0).astype(BF16)

    for step in X_ORDER:
        x = (xi + step) % NX
        wait_block(x, 0)
        for distance in NEAR:
            slot = SLOTS.index(distance)
            target = dp_at(z_peer[(NZ - distance) % NZ], group)
            remote(blocks(x, 0, 1), blocks(x, slot, 1), target, block_sem.at[x, slot]).start()
    for number in range(len(WAVES)):
        for distance in WAVES[number]:
            wait_block(xi, SLOTS.index(distance))
        for step in X_ORDER:
            wave(xi, number, dp_at(zi, x_peer[step])).start()
    for distance in NEAR:
        wait_block(xi, SLOTS.index(distance))
    lay_out(0, xi)
    relay(xi).start()
    for place, step in enumerate(X_ORDER):
        x = (xi + step) % NX
        for distance in NEAR:
            wait_block(x, SLOTS.index(distance))
        for number in range(len(WAVES)):
            wave(x, number, mate).wait_recv()
        lay_out(1 + place, x)
        relay(x).start()

    own_seqs = seqs // 2
    tile = feats[:own_seqs]
    inner_own = dot_nt(jnp.concatenate([tile, lhs_query[...]], axis=0), tile)
    for step in (0,) + X_ORDER:
        relay((xi + step) % NX).wait_recv()
    other = feats[own_seqs:]
    inner_other = dot_nt(jnp.concatenate([feats[...], lhs_query[...]], axis=0), other)
    cross = inner_other[:own_seqs]
    kmat = jnp.concatenate(
        [
            jnp.concatenate([inner_own[:own_seqs], cross], axis=1),
            jnp.concatenate([cross.T, inner_other[own_seqs:seqs]], axis=1),
        ],
        axis=0,
    )
    u = jnp.concatenate(
        [
            inner_own[own_seqs:own_seqs + 16] + inner_own[own_seqs + 16:],
            inner_other[seqs:seqs + 16] + inner_other[seqs + 16:],
        ],
        axis=1,
    )
    eye = lax.broadcasted_iota(jnp.int32, (seqs, seqs), 0) == lax.broadcasted_iota(jnp.int32, (seqs, seqs), 1)
    trace = jnp.sum(jnp.sum(jnp.where(eye, kmat, 0.0), axis=1, keepdims=True), axis=0, keepdims=True)
    damping = 0.1 * trace / (rows * 2 * rank)
    k_high, k_low = high_low(kmat)
    k_both = jnp.concatenate([k_high, k_low], axis=1)

    def apply_k(v):
        v_high, v_low = high_low(v)
        out = dot_nn(jnp.concatenate([v_high, v_low], axis=0), k_both)
        return out[:16, :seqs] + (out[:16, seqs:] + out[16:, :seqs])

    w, v = u, u
    y = jnp.zeros_like(u)
    y_dir = jnp.zeros_like(u)
    c = jnp.ones_like(query_sq)
    c_dir = jnp.ones_like(query_sq)
    resid_sq, dir_sq = query_sq, query_sq
    scores = jnp.zeros_like(u)
    selfterm = jnp.zeros_like(query_sq)
    for iteration in range(ITERS):
        alpha = resid_sq / (jnp.sum(v * v, axis=1, keepdims=True) + damping * dir_sq)
        scores = scores + alpha * v
        selfterm = selfterm + alpha * resid_sq
        if iteration == ITERS - 1:
            break
        image = apply_k(v) + damping * v
        w = w - alpha * image
        y = y - alpha * (v + damping * y_dir)
        c = c - alpha * damping * c_dir
        next_sq = c * c * query_sq + jnp.sum(y * (c * u + w), axis=1, keepdims=True)
        beta = next_sq / resid_sq
        v = w + beta * v
        y_dir = y + beta * y_dir
        c_dir = c + beta * c_dir
        dir_sq = next_sq + beta * beta * dir_sq
        resid_sq = next_sq

    s_high, s_low = high_low(scores)
    s_last = (scores - s_high.astype(F32) - s_low.astype(F32)).astype(BF16)
    picked = dot_nn(jnp.concatenate([s_high, s_low, s_last], axis=0), pick[...])
    picked = picked[:16] + picked[16:32] + picked[32:]
    part_col = lax.broadcasted_iota(jnp.int32, (16, 128), 1)
    parts[mp] = jnp.where(part_col == 2 * cands, selfterm, picked)
    for step in range(1, modules):
        pltpu.make_async_remote_copy(
            src_ref=parts.at[mp], dst_ref=parts.at[mp], send_sem=part_send, recv_sem=part_sem.at[mp],
            device_id={"mp": m_peer[step]}, device_id_type=MESH,
        ).start()

    own_tile = feats[:, pl.ds(pl.multiple_of((dp // 2) * 128, 128), 128)].astype(F32).T
    own_rows = jnp.where(dp % 2 == 0, own_tile[:rank], own_tile[rank:]).astype(BF16)
    gram_chunks = 4
    gram_width = gram_ref.shape[1] // gram_chunks
    for chunk in range(gram_chunks):
        cols = slice(chunk * gram_width, (chunk + 1) * gram_width)
        gram_ref[:, cols] = dot_nn(own_rows, feats[:, cols])

    for step in range(1, modules):
        other = m_peer[step]
        pltpu.make_async_remote_copy(
            src_ref=parts.at[other], dst_ref=parts.at[other], send_sem=part_send, recv_sem=part_sem.at[other],
            device_id={"mp": other}, device_id_type=MESH,
        ).wait_recv()
    total = parts[0]
    for m in range(1, modules):
        total = total + parts[m]
    infl_ref[...] = total[:, :2 * cands] / jnp.sqrt(total[:, 2 * cands:2 * cands + 1])

    def all_sent(ref, count, sem):
        pltpu.make_async_remote_copy(
            src_ref=ref.at[pl.ds(0, count)], dst_ref=ref.at[pl.ds(0, count)], send_sem=sem, recv_sem=relay_sem.at[0],
            device_id=mate, device_id_type=MESH,
        ).wait_send()

    own_copies = (NX - 1) + (NZ - 1) + len(NEAR) * (NX - 1)
    wave_copies = sum(len(distances) for distances in WAVES) * (NX - 1)
    all_sent(raw, own_copies + wave_copies, send_sem)
    all_sent(feats, seqs // 2, relay_send)
    all_sent(parts, modules - 1, part_send)


def write_kernel(gram_ref, infl_ref, gram_out, infl_out, gram_sem, infl_sem):
    gram_copy = pltpu.make_async_copy(gram_ref, gram_out, gram_sem)
    infl_copy = pltpu.make_async_copy(infl_ref, infl_out, infl_sem)
    gram_copy.start()
    infl_copy.start()
    infl_copy.wait()
    gram_copy.wait()


def on_device(activations, out_grads, proj_in, proj_out, query_feat, candidates):
    _, seqs, tokens, depth = activations.shape
    rank = proj_in.shape[1]
    queries, size = query_feat.shape[1:]
    modules = lax.axis_size("mp")
    shards = lax.axis_size("dp")
    total = shards * seqs
    vmem = pltpu.VMEM
    dma = pltpu.SemaphoreType.DMA
    gram, influence = pl.pallas_call(
        kernel,
        name="influence",
        out_shape=(
            jax.ShapeDtypeStruct((size // shards, size), F32),
            jax.ShapeDtypeStruct((queries, candidates.shape[1] * seqs), F32),
        ),
        in_specs=[pl.BlockSpec(memory_space=pltpu.HBM)] * 6,
        out_specs=(pl.BlockSpec(memory_space=pltpu.VMEM), pl.BlockSpec(memory_space=pltpu.VMEM)),
        scratch_shapes=[
            pltpu.SMEM(candidates.shape, jnp.int32),
            vmem((seqs * tokens, depth), BF16),
            vmem((seqs * tokens, depth), BF16),
            vmem((rank, depth), BF16),
            vmem((rank, depth), BF16),
            vmem((queries, size), F32),
            vmem((NX * NZ, seqs * size // 128, 128), BF16),
            vmem((total // NC * size // 128, 128), F32),
            vmem((total, size), BF16),
            vmem((rank, seqs * tokens), F32),
            vmem((2 * queries, size), BF16),
            vmem((total, 128), BF16),
            vmem((modules, queries, 128), F32),
            dma((CHUNKS, 4)),
            dma,
            dma,
            dma,
            dma,
            dma((NX, NZ)),
            dma((NX, len(WAVES))),
            dma((NX,)),
            dma,
            dma((modules,)),
        ],
        compiler_params=pltpu.CompilerParams(
            collective_id=0, has_side_effects=True, vmem_limit_bytes=48 * 2**20
        ),
    )(
        *(
            pltpu.with_memory_space_constraint(operand, pltpu.HBM)
            for operand in (
                candidates,
                activations.reshape(seqs * tokens, depth),
                out_grads.reshape(seqs * tokens, depth),
                proj_in.reshape(rank, depth),
                proj_out.reshape(rank, depth),
                query_feat.reshape(queries, size),
            )
        ),
    )
    gram, influence = pl.pallas_call(
        write_kernel,
        name="write",
        out_shape=(jax.ShapeDtypeStruct(gram.shape, F32), jax.ShapeDtypeStruct(influence.shape, F32)),
        in_specs=[pl.BlockSpec(memory_space=pltpu.VMEM)] * 2,
        out_specs=[pl.BlockSpec(memory_space=pltpu.HBM)] * 2,
        scratch_shapes=[dma, dma],
        compiler_params=pltpu.CompilerParams(vmem_limit_bytes=2**20),
    )(gram, influence)
    return gram[None], influence


def solution(mesh):
    placed = (
        P("mp", "dp", None, None),
        P("mp", "dp", None, None),
        P("mp", None, None),
        P("mp", None, None),
        P("mp", "dp", None),
        P("dp", None),
    )
    return jax.shard_map(
        on_device,
        mesh=mesh,
        in_specs=placed,
        out_specs=(P("mp", "dp", None), P("dp", None)),
        check_vma=False,
    )
```

```python
import functools

import jax
import jax.numpy as jnp
from jax import lax
from jax.experimental import pallas as pl
from jax.experimental.pallas import tpu as pltpu
from jax.sharding import PartitionSpec as P

ITERS = 6
NZ, NX, NC = 8, 4, 2
GROUPS = NX * NC
CHUNKS = 4
MESH = pl.DeviceIdType.MESH
F32 = jnp.float32
BF16 = jnp.bfloat16
X_ORDER = (2, 1, 3)
SLOTS = (0, 1, 7, 2, 6, 3, 5, 4)
NEAR = (1, 7)
WAVES = ((2, 6, 3, 5, 4),)


def dot_nt(lhs, rhs):
    return lax.dot_general(lhs, rhs, (((1,), (1,)), ((), ())), preferred_element_type=F32)


def dot_nn(lhs, rhs):
    return jnp.dot(lhs, rhs, preferred_element_type=F32)


def high_low(value):
    high = value.astype(BF16)
    return high, (value - high.astype(F32)).astype(BF16)


def kernel(
    cand_hbm, act_hbm, grad_hbm, pin_hbm, pout_hbm, query_hbm,
    gram_ref, infl_ref,
    cand, act, grad, pin, pout, query, raw, wide, feats, turned, lhs_query, pick, parts,
    in_sem, query_sem, cand_sem, send_sem, relay_send, block_sem, wave_sem, relay_sem, part_send, part_sem,
):
    dp = lax.axis_index("dp")
    mp = lax.axis_index("mp")
    modules = parts.shape[0]
    zi, group = dp // GROUPS, dp % GROUPS
    xi, core = group // NC, group % NC

    width = act.shape[1] // CHUNKS
    loads = []
    for chunk in range(CHUNKS):
        cols = pl.ds(chunk * width, width)
        row = []
        for which, (src, dst) in enumerate(((pout_hbm, pout), (grad_hbm, grad), (pin_hbm, pin), (act_hbm, act))):
            row.append(pltpu.make_async_copy(src.at[:, cols], dst.at[:, cols], in_sem.at[chunk, which]))
        loads.append(row)
        for copy in row:
            copy.start()
    query_load = pltpu.make_async_copy(query_hbm, query, query_sem)
    query_load.start()
    cand_load = pltpu.make_async_copy(cand_hbm, cand, cand_sem)
    cand_load.start()

    def dp_at(z, g):
        return {"dp": z * GROUPS + g}

    mate = dp_at(zi, xi * NC + (1 - core))
    z_peer = [(zi + step) % NZ for step in range(NZ)]
    x_peer = [((xi + step) % NX) * NC + core for step in range(NX)]
    m_peer = [(mp + step) % modules for step in range(modules)]

    barrier = pltpu.get_barrier_semaphore()
    for step in range(1, NZ):
        pl.semaphore_signal(barrier, 1, device_id=dp_at(z_peer[step], group), device_id_type=MESH)
    for step in range(1, NX):
        pl.semaphore_signal(barrier, 1, device_id=dp_at(zi, x_peer[step]), device_id_type=MESH)
    pl.semaphore_signal(barrier, 1, device_id=mate, device_id_type=MESH)
    for step in range(1, modules):
        pl.semaphore_signal(barrier, 1, device_id={"mp": m_peer[step]}, device_id_type=MESH)

    gout = jnp.zeros((pout.shape[0], grad.shape[0]), F32)
    xin = jnp.zeros((act.shape[0], 2 * pin.shape[0]), F32)
    for chunk in range(CHUNKS):
        cols = slice(chunk * width, (chunk + 1) * width)
        loads[chunk][0].wait()
        loads[chunk][1].wait()
        gout += dot_nt(pout[:, cols], grad[:, cols])
        loads[chunk][2].wait()
        loads[chunk][3].wait()
        pin_cols = pin[:, cols]
        xin += dot_nt(act[:, cols], jnp.concatenate([pin_cols, pin_cols], axis=0))

    rank = pout.shape[0]
    half = rank // 2
    turned[...] = gout
    stacked = jnp.concatenate(
        [turned[pl.ds(0, half, stride=2), :], turned[pl.ds(1, half, stride=2), :]], axis=0
    ).astype(BF16)
    token = lax.broadcasted_iota(jnp.int32, xin.shape, 0)
    tokens = act.shape[0] // 2
    both = jnp.concatenate(
        [jnp.where(token < tokens, xin, 0.0), jnp.where(token >= tokens, xin, 0.0)], axis=1
    ).astype(BF16)
    joined = dot_nn(stacked, both)
    lane = lax.broadcasted_iota(jnp.int32, (half, 2 * rank), 1)
    own = [
        jnp.where(lane < rank, joined[:half, s * 2 * rank:(s + 1) * 2 * rank], joined[half:, s * 2 * rank:(s + 1) * 2 * rank])
        for s in range(2)
    ]
    raw[xi * NZ] = jnp.concatenate(own, axis=0).astype(BF16)

    pl.semaphore_wait(barrier, (NZ - 1) + (NX - 1) + 1 + (modules - 1))

    rows = half
    seqs = GROUPS * NZ * 2
    group_rows = NZ * 2 * rows
    group_seqs = NZ * 2

    def seqs_of(x, other):
        return pl.ds(pl.multiple_of(other * (seqs // 2) + x * group_seqs, group_seqs), group_seqs)

    def lay_out(place, x):
        base = place * group_rows
        wide[base:base + group_rows] = raw[pl.ds(x * NZ, NZ)].reshape(group_rows, 2 * rank).astype(F32)
        for r in range(rows):
            feats[seqs_of(x, 0), r * 128:(r + 1) * 128] = wide[pl.ds(base + r, group_seqs, stride=rows), :].astype(BF16)

    def remote(src, dst, target, arrival):
        return pltpu.make_async_remote_copy(
            src_ref=src, dst_ref=dst, send_sem=send_sem, recv_sem=arrival, device_id=target, device_id_type=MESH
        )

    def blocks(x, first, count):
        return raw.at[pl.ds(x * NZ + first, count)]

    def send_own(distance, step):
        slot = SLOTS.index(distance)
        target = dp_at(z_peer[(NZ - distance) % NZ], x_peer[step])
        remote(blocks(xi, 0, 1), blocks(xi, slot, 1), target, block_sem.at[xi, slot]).start()

    def wait_block(x, slot):
        remote(blocks(x, slot, 1), blocks(x, slot, 1), mate, block_sem.at[x, slot]).wait_recv()

    def wave(x, number, target):
        slots = [SLOTS.index(distance) for distance in WAVES[number]]
        at = blocks(x, slots[0], len(slots))
        return remote(at, at, target, wave_sem.at[x, number])

    def relay(x):
        return pltpu.make_async_remote_copy(
            src_ref=feats.at[seqs_of(x, 0)], dst_ref=feats.at[seqs_of(x, 1)], send_sem=relay_send,
            recv_sem=relay_sem.at[x], device_id=mate, device_id_type=MESH,
        )

    for step in X_ORDER:
        send_own(0, step)
    for distance in (4, 3, 5, 2, 6, 1, 7):
        send_own(distance, 0)
    query_load.wait()
    cand_load.wait()
    query_high, query_low = high_low(query[...])
    lhs_query[:16, :] = query_high
    lhs_query[16:, :] = query_low
    query_norm = jnp.sum(query[...] * query[...], axis=1, keepdims=True)
    query_sq = jnp.broadcast_to(query_norm, (16, 128)).T[:1]

    col = lax.broadcasted_iota(jnp.int32, (seqs, 128), 1)
    spot = jnp.full((seqs, 128), -1, jnp.int32)
    cands = cand.shape[1]
    for i in range(cands):
        shard = cand[0, i]
        distance = (shard // GROUPS + NZ - zi) % NZ
        slot = 0
        for number in range(1, NZ):
            slot = jnp.where(distance == SLOTS[number], number, slot)
        place = shard % GROUPS
        first = (place % NC + NC - core) % NC * (seqs // 2) + place // NC * group_seqs + slot * 2
        spot = jnp.where(col // 2 == i, first + col % 2, spot)
    pick[...] = jnp.where(lax.broadcasted_iota(jnp.int32, (seqs, 128), 0) == spot, 1.0, 0.0).astype(BF16)

    for step in X_ORDER:
        x = (xi + step) % NX
        wait_block(x, 0)
        for distance in NEAR:
            slot = SLOTS.index(distance)
            target = dp_at(z_peer[(NZ - distance) % NZ], group)
            remote(blocks(x, 0, 1), blocks(x, slot, 1), target, block_sem.at[x, slot]).start()
    for number in range(len(WAVES)):
        for distance in WAVES[number]:
            wait_block(xi, SLOTS.index(distance))
        for step in X_ORDER:
            wave(xi, number, dp_at(zi, x_peer[step])).start()
    for distance in NEAR:
        wait_block(xi, SLOTS.index(distance))
    lay_out(0, xi)
    relay(xi).start()
    for place, step in enumerate(X_ORDER):
        x = (xi + step) % NX
        for distance in NEAR:
            wait_block(x, SLOTS.index(distance))
        for number in range(len(WAVES)):
            wave(x, number, mate).wait_recv()
        lay_out(1 + place, x)
        relay(x).start()

    own_seqs = seqs // 2
    tile = feats[:own_seqs]
    inner_own = dot_nt(jnp.concatenate([tile, lhs_query[...]], axis=0), tile)
    for step in (0,) + X_ORDER:
        relay((xi + step) % NX).wait_recv()
    other = feats[own_seqs:]
    inner_other = dot_nt(jnp.concatenate([feats[...], lhs_query[...]], axis=0), other)
    cross = inner_other[:own_seqs]
    kmat = jnp.concatenate(
        [
            jnp.concatenate([inner_own[:own_seqs], cross], axis=1),
            jnp.concatenate([cross.T, inner_other[own_seqs:seqs]], axis=1),
        ],
        axis=0,
    )
    u = jnp.concatenate(
        [
            inner_own[own_seqs:own_seqs + 16] + inner_own[own_seqs + 16:],
            inner_other[seqs:seqs + 16] + inner_other[seqs + 16:],
        ],
        axis=1,
    )
    eye = lax.broadcasted_iota(jnp.int32, (seqs, seqs), 0) == lax.broadcasted_iota(jnp.int32, (seqs, seqs), 1)
    trace = jnp.sum(jnp.sum(jnp.where(eye, kmat, 0.0), axis=1, keepdims=True), axis=0, keepdims=True)
    damping = 0.1 * trace / (rows * 2 * rank)
    k_high, k_low = high_low(kmat)
    k_both = jnp.concatenate([k_high, k_low], axis=0)

    def apply_k(v):
        v_high, v_low = high_low(v)
        out = dot_nn(k_both, v_high)
        return out[:seqs] + (out[seqs:] + dot_nn(k_high, v_low))

    def over_seqs(terms):
        return jnp.sum(terms, axis=0, keepdims=True)

    u = u.T
    w, v = u, u
    y = jnp.zeros_like(u)
    y_dir = jnp.zeros_like(u)
    c = jnp.ones_like(query_sq)
    c_dir = jnp.ones_like(query_sq)
    resid_sq, dir_sq = query_sq, query_sq
    scores = jnp.zeros_like(u)
    selfterm = jnp.zeros_like(query_sq)
    for iteration in range(ITERS):
        alpha = resid_sq / (over_seqs(v * v) + damping * dir_sq)
        scores = scores + alpha * v
        selfterm = selfterm + alpha * resid_sq
        if iteration == ITERS - 1:
            break
        image = apply_k(v) + damping * v
        w = w - alpha * image
        y = y - alpha * (v + damping * y_dir)
        c = c - alpha * damping * c_dir
        next_sq = c * c * query_sq + over_seqs(y * (c * u + w))
        beta = next_sq / resid_sq
        v = w + beta * v
        y_dir = y + beta * y_dir
        c_dir = c + beta * c_dir
        dir_sq = next_sq + beta * beta * dir_sq
        resid_sq = next_sq

    scores = scores.T
    selfterm = jnp.broadcast_to(selfterm, (128, 16)).T
    s_high, s_low = high_low(scores)
    s_last = (scores - s_high.astype(F32) - s_low.astype(F32)).astype(BF16)
    picked = dot_nn(jnp.concatenate([s_high, s_low, s_last], axis=0), pick[...])
    picked = picked[:16] + picked[16:32] + picked[32:]
    part_col = lax.broadcasted_iota(jnp.int32, (16, 128), 1)
    parts[mp] = jnp.where(part_col == 2 * cands, selfterm, picked)
    for step in range(1, modules):
        pltpu.make_async_remote_copy(
            src_ref=parts.at[mp], dst_ref=parts.at[mp], send_sem=part_send, recv_sem=part_sem.at[mp],
            device_id={"mp": m_peer[step]}, device_id_type=MESH,
        ).start()

    own_tile = feats[:, pl.ds(pl.multiple_of((dp // 2) * 128, 128), 128)].astype(F32).T
    own_rows = jnp.where(dp % 2 == 0, own_tile[:rank], own_tile[rank:]).astype(BF16)
    gram_chunks = 4
    gram_width = gram_ref.shape[1] // gram_chunks
    for chunk in range(gram_chunks):
        cols = slice(chunk * gram_width, (chunk + 1) * gram_width)
        gram_ref[:, cols] = dot_nn(own_rows, feats[:, cols])

    for step in range(1, modules):
        other = m_peer[step]
        pltpu.make_async_remote_copy(
            src_ref=parts.at[other], dst_ref=parts.at[other], send_sem=part_send, recv_sem=part_sem.at[other],
            device_id={"mp": other}, device_id_type=MESH,
        ).wait_recv()
    total = parts[0]
    for m in range(1, modules):
        total = total + parts[m]
    infl_ref[...] = total[:, :2 * cands] / jnp.sqrt(total[:, 2 * cands:2 * cands + 1])

    def all_sent(ref, count, sem):
        pltpu.make_async_remote_copy(
            src_ref=ref.at[pl.ds(0, count)], dst_ref=ref.at[pl.ds(0, count)], send_sem=sem, recv_sem=relay_sem.at[0],
            device_id=mate, device_id_type=MESH,
        ).wait_send()

    own_copies = (NX - 1) + (NZ - 1) + len(NEAR) * (NX - 1)
    wave_copies = sum(len(distances) for distances in WAVES) * (NX - 1)
    all_sent(raw, own_copies + wave_copies, send_sem)
    all_sent(feats, seqs // 2, relay_send)
    all_sent(parts, modules - 1, part_send)


def write_kernel(gram_ref, infl_ref, gram_out, infl_out, gram_sem, infl_sem):
    gram_copy = pltpu.make_async_copy(gram_ref, gram_out, gram_sem)
    infl_copy = pltpu.make_async_copy(infl_ref, infl_out, infl_sem)
    gram_copy.start()
    infl_copy.start()
    infl_copy.wait()
    gram_copy.wait()


def on_device(activations, out_grads, proj_in, proj_out, query_feat, candidates):
    _, seqs, tokens, depth = activations.shape
    rank = proj_in.shape[1]
    queries, size = query_feat.shape[1:]
    modules = lax.axis_size("mp")
    shards = lax.axis_size("dp")
    total = shards * seqs
    vmem = pltpu.VMEM
    dma = pltpu.SemaphoreType.DMA
    gram, influence = pl.pallas_call(
        kernel,
        name="influence",
        out_shape=(
            jax.ShapeDtypeStruct((size // shards, size), F32),
            jax.ShapeDtypeStruct((queries, candidates.shape[1] * seqs), F32),
        ),
        in_specs=[pl.BlockSpec(memory_space=pltpu.HBM)] * 6,
        out_specs=(pl.BlockSpec(memory_space=pltpu.VMEM), pl.BlockSpec(memory_space=pltpu.VMEM)),
        scratch_shapes=[
            pltpu.SMEM(candidates.shape, jnp.int32),
            vmem((seqs * tokens, depth), BF16),
            vmem((seqs * tokens, depth), BF16),
            vmem((rank, depth), BF16),
            vmem((rank, depth), BF16),
            vmem((queries, size), F32),
            vmem((NX * NZ, seqs * size // 128, 128), BF16),
            vmem((total // NC * size // 128, 128), F32),
            vmem((total, size), BF16),
            vmem((rank, seqs * tokens), F32),
            vmem((2 * queries, size), BF16),
            vmem((total, 128), BF16),
            vmem((modules, queries, 128), F32),
            dma((CHUNKS, 4)),
            dma,
            dma,
            dma,
            dma,
            dma((NX, NZ)),
            dma((NX, len(WAVES))),
            dma((NX,)),
            dma,
            dma((modules,)),
        ],
        compiler_params=pltpu.CompilerParams(
            collective_id=0, has_side_effects=True, vmem_limit_bytes=48 * 2**20
        ),
    )(
        *(
            pltpu.with_memory_space_constraint(operand, pltpu.HBM)
            for operand in (
                candidates,
                activations.reshape(seqs * tokens, depth),
                out_grads.reshape(seqs * tokens, depth),
                proj_in.reshape(rank, depth),
                proj_out.reshape(rank, depth),
                query_feat.reshape(queries, size),
            )
        ),
    )
    gram, influence = pl.pallas_call(
        write_kernel,
        name="write",
        out_shape=(jax.ShapeDtypeStruct(gram.shape, F32), jax.ShapeDtypeStruct(influence.shape, F32)),
        in_specs=[pl.BlockSpec(memory_space=pltpu.VMEM)] * 2,
        out_specs=[pl.BlockSpec(memory_space=pltpu.HBM)] * 2,
        scratch_shapes=[dma, dma],
        compiler_params=pltpu.CompilerParams(vmem_limit_bytes=2**20),
    )(gram, influence)
    return gram[None], influence


def solution(mesh):
    placed = (
        P("mp", "dp", None, None),
        P("mp", "dp", None, None),
        P("mp", None, None),
        P("mp", None, None),
        P("mp", "dp", None),
        P("dp", None),
    )
    return jax.shard_map(
        on_device,
        mesh=mesh,
        in_specs=placed,
        out_specs=(P("mp", "dp", None), P("dp", None)),
        check_vma=False,
    )
```

```python
import functools

import jax
import jax.numpy as jnp
from jax import lax
from jax.experimental import pallas as pl
from jax.experimental.pallas import tpu as pltpu
from jax.sharding import PartitionSpec as P

ITERS = 6
NZ, NX, NC = 8, 4, 2
GROUPS = NX * NC
CHUNKS = 4
MESH = pl.DeviceIdType.MESH
F32 = jnp.float32
BF16 = jnp.bfloat16
X_ORDER = (2, 1, 3)
SLOTS = (0, 1, 7, 2, 6, 3, 5, 4)
NEAR = (1, 7)
WAVES = ((2, 6, 3, 5, 4),)


def dot_nt(lhs, rhs):
    return lax.dot_general(lhs, rhs, (((1,), (1,)), ((), ())), preferred_element_type=F32)


def dot_nn(lhs, rhs):
    return jnp.dot(lhs, rhs, preferred_element_type=F32)


def high_low(value):
    high = value.astype(BF16)
    return high, (value - high.astype(F32)).astype(BF16)


def kernel(
    cand_hbm, act_hbm, grad_hbm, pin_hbm, pout_hbm, query_hbm,
    gram_ref, infl_ref,
    cand, act, grad, pin, pout, query, raw, wide, feats, turned, lhs_query, pick, parts,
    in_sem, query_sem, cand_sem, send_sem, relay_send, block_sem, wave_sem, relay_sem, part_send, part_sem,
):
    dp = lax.axis_index("dp")
    mp = lax.axis_index("mp")
    modules = parts.shape[0]
    zi, group = dp // GROUPS, dp % GROUPS
    xi, core = group // NC, group % NC

    width = act.shape[1] // CHUNKS
    loads = []
    for chunk in range(CHUNKS):
        cols = pl.ds(chunk * width, width)
        row = []
        for which, (src, dst) in enumerate(((pout_hbm, pout), (grad_hbm, grad), (pin_hbm, pin), (act_hbm, act))):
            row.append(pltpu.make_async_copy(src.at[:, cols], dst.at[:, cols], in_sem.at[chunk, which]))
        loads.append(row)
        for copy in row:
            copy.start()
    query_load = pltpu.make_async_copy(query_hbm, query, query_sem)
    cand_load = pltpu.make_async_copy(cand_hbm, cand, cand_sem)

    def dp_at(z, g):
        return {"dp": z * GROUPS + g}

    mate = dp_at(zi, xi * NC + (1 - core))
    z_peer = [(zi + step) % NZ for step in range(NZ)]
    x_peer = [((xi + step) % NX) * NC + core for step in range(NX)]
    m_peer = [(mp + step) % modules for step in range(modules)]

    barrier = pltpu.get_barrier_semaphore()
    for step in range(1, NZ):
        pl.semaphore_signal(barrier, 1, device_id=dp_at(z_peer[step], group), device_id_type=MESH)
    for step in range(1, NX):
        pl.semaphore_signal(barrier, 1, device_id=dp_at(zi, x_peer[step]), device_id_type=MESH)
    pl.semaphore_signal(barrier, 1, device_id=mate, device_id_type=MESH)
    for step in range(1, modules):
        pl.semaphore_signal(barrier, 1, device_id={"mp": m_peer[step]}, device_id_type=MESH)

    gout = jnp.zeros((pout.shape[0], grad.shape[0]), F32)
    xin = jnp.zeros((act.shape[0], 2 * pin.shape[0]), F32)
    for chunk in range(CHUNKS):
        cols = slice(chunk * width, (chunk + 1) * width)
        loads[chunk][0].wait()
        loads[chunk][1].wait()
        gout += dot_nt(pout[:, cols], grad[:, cols])
        loads[chunk][2].wait()
        loads[chunk][3].wait()
        pin_cols = pin[:, cols]
        xin += dot_nt(act[:, cols], jnp.concatenate([pin_cols, pin_cols], axis=0))

    query_load.start()
    cand_load.start()

    rank = pout.shape[0]
    half = rank // 2
    turned[...] = gout
    stacked = jnp.concatenate(
        [turned[pl.ds(0, half, stride=2), :], turned[pl.ds(1, half, stride=2), :]], axis=0
    ).astype(BF16)
    token = lax.broadcasted_iota(jnp.int32, xin.shape, 0)
    tokens = act.shape[0] // 2
    both = jnp.concatenate(
        [jnp.where(token < tokens, xin, 0.0), jnp.where(token >= tokens, xin, 0.0)], axis=1
    ).astype(BF16)
    joined = dot_nn(stacked, both)
    lane = lax.broadcasted_iota(jnp.int32, (half, 2 * rank), 1)
    own = [
        jnp.where(lane < rank, joined[:half, s * 2 * rank:(s + 1) * 2 * rank], joined[half:, s * 2 * rank:(s + 1) * 2 * rank])
        for s in range(2)
    ]
    raw[xi * NZ] = jnp.concatenate(own, axis=0).astype(BF16)

    pl.semaphore_wait(barrier, (NZ - 1) + (NX - 1) + 1 + (modules - 1))

    rows = half
    seqs = GROUPS * NZ * 2
    group_rows = NZ * 2 * rows
    group_seqs = NZ * 2

    def seqs_of(x, other):
        return pl.ds(pl.multiple_of(other * (seqs // 2) + x * group_seqs, group_seqs), group_seqs)

    def lay_out(place, x):
        base = place * group_rows
        wide[base:base + group_rows] = raw[pl.ds(x * NZ, NZ)].reshape(group_rows, 2 * rank).astype(F32)
        for r in range(rows):
            feats[seqs_of(x, 0), r * 128:(r + 1) * 128] = wide[pl.ds(base + r, group_seqs, stride=rows), :].astype(BF16)

    def remote(src, dst, target, arrival):
        return pltpu.make_async_remote_copy(
            src_ref=src, dst_ref=dst, send_sem=send_sem, recv_sem=arrival, device_id=target, device_id_type=MESH
        )

    def blocks(x, first, count):
        return raw.at[pl.ds(x * NZ + first, count)]

    def send_own(distance, step):
        slot = SLOTS.index(distance)
        target = dp_at(z_peer[(NZ - distance) % NZ], x_peer[step])
        remote(blocks(xi, 0, 1), blocks(xi, slot, 1), target, block_sem.at[xi, slot]).start()

    def wait_block(x, slot):
        remote(blocks(x, slot, 1), blocks(x, slot, 1), mate, block_sem.at[x, slot]).wait_recv()

    def wave(x, number, target):
        slots = [SLOTS.index(distance) for distance in WAVES[number]]
        at = blocks(x, slots[0], len(slots))
        return remote(at, at, target, wave_sem.at[x, number])

    def relay(x):
        return pltpu.make_async_remote_copy(
            src_ref=feats.at[seqs_of(x, 0)], dst_ref=feats.at[seqs_of(x, 1)], send_sem=relay_send,
            recv_sem=relay_sem.at[x], device_id=mate, device_id_type=MESH,
        )

    for step in X_ORDER:
        send_own(0, step)
    for distance in (1, 7, 2, 6, 3, 5, 4):
        send_own(distance, 0)
    query_load.wait()
    cand_load.wait()
    query_high, query_low = high_low(query[...])
    lhs_query[:16, :] = query_high
    lhs_query[16:, :] = query_low
    query_norm = jnp.sum(query[...] * query[...], axis=1, keepdims=True)
    query_sq = jnp.broadcast_to(query_norm, (16, 128)).T[:1]

    col = lax.broadcasted_iota(jnp.int32, (seqs, 128), 1)
    spot = jnp.full((seqs, 128), -1, jnp.int32)
    cands = cand.shape[1]
    for i in range(cands):
        shard = cand[0, i]
        distance = (shard // GROUPS + NZ - zi) % NZ
        slot = 0
        for number in range(1, NZ):
            slot = jnp.where(distance == SLOTS[number], number, slot)
        place = shard % GROUPS
        first = (place % NC + NC - core) % NC * (seqs // 2) + place // NC * group_seqs + slot * 2
        spot = jnp.where(col // 2 == i, first + col % 2, spot)
    pick[...] = jnp.where(lax.broadcasted_iota(jnp.int32, (seqs, 128), 0) == spot, 1.0, 0.0).astype(BF16)

    for step in X_ORDER:
        x = (xi + step) % NX
        wait_block(x, 0)
        for distance in NEAR:
            slot = SLOTS.index(distance)
            target = dp_at(z_peer[(NZ - distance) % NZ], group)
            remote(blocks(x, 0, 1), blocks(x, slot, 1), target, block_sem.at[x, slot]).start()
    for number in range(len(WAVES)):
        for distance in WAVES[number]:
            wait_block(xi, SLOTS.index(distance))
        for step in X_ORDER:
            wave(xi, number, dp_at(zi, x_peer[step])).start()
    for distance in NEAR:
        wait_block(xi, SLOTS.index(distance))
    lay_out(0, xi)
    relay(xi).start()
    for place, step in enumerate(X_ORDER):
        x = (xi + step) % NX
        for distance in NEAR:
            wait_block(x, SLOTS.index(distance))
        for number in range(len(WAVES)):
            wave(x, number, mate).wait_recv()
        lay_out(1 + place, x)
        relay(x).start()

    own_seqs = seqs // 2
    tile = feats[:own_seqs]
    inner_own = dot_nt(jnp.concatenate([tile, lhs_query[...]], axis=0), tile)
    for step in (0,) + X_ORDER:
        relay((xi + step) % NX).wait_recv()
    other = feats[own_seqs:]
    inner_other = dot_nt(jnp.concatenate([feats[...], lhs_query[...]], axis=0), other)
    cross = inner_other[:own_seqs]
    kmat = jnp.concatenate(
        [
            jnp.concatenate([inner_own[:own_seqs], cross], axis=1),
            jnp.concatenate([cross.T, inner_other[own_seqs:seqs]], axis=1),
        ],
        axis=0,
    )
    u = jnp.concatenate(
        [
            inner_own[own_seqs:own_seqs + 16] + inner_own[own_seqs + 16:],
            inner_other[seqs:seqs + 16] + inner_other[seqs + 16:],
        ],
        axis=1,
    )
    eye = lax.broadcasted_iota(jnp.int32, (seqs, seqs), 0) == lax.broadcasted_iota(jnp.int32, (seqs, seqs), 1)
    trace = jnp.sum(jnp.sum(jnp.where(eye, kmat, 0.0), axis=1, keepdims=True), axis=0, keepdims=True)
    damping = 0.1 * trace / (rows * 2 * rank)
    k_high, k_low = high_low(kmat)
    k_both = jnp.concatenate([k_high, k_low], axis=0)

    def apply_k(v):
        v_high, v_low = high_low(v)
        out = dot_nn(k_both, v_high)
        return out[:seqs] + (out[seqs:] + dot_nn(k_high, v_low))

    def over_seqs(terms):
        return jnp.sum(terms, axis=0, keepdims=True)

    u = u.T
    w, v = u, u
    y = jnp.zeros_like(u)
    y_dir = jnp.zeros_like(u)
    c = jnp.ones_like(query_sq)
    c_dir = jnp.ones_like(query_sq)
    resid_sq, dir_sq = query_sq, query_sq
    scores = jnp.zeros_like(u)
    selfterm = jnp.zeros_like(query_sq)
    for iteration in range(ITERS):
        alpha = resid_sq / (over_seqs(v * v) + damping * dir_sq)
        scores = scores + alpha * v
        selfterm = selfterm + alpha * resid_sq
        if iteration == ITERS - 1:
            break
        image = apply_k(v) + damping * v
        w = w - alpha * image
        y = y - alpha * (v + damping * y_dir)
        c = c - alpha * damping * c_dir
        next_sq = c * c * query_sq + over_seqs(y * (c * u + w))
        beta = next_sq / resid_sq
        v = w + beta * v
        y_dir = y + beta * y_dir
        c_dir = c + beta * c_dir
        dir_sq = next_sq + beta * beta * dir_sq
        resid_sq = next_sq

    scores = scores.T
    selfterm = jnp.broadcast_to(selfterm, (128, 16)).T
    s_high, s_low = high_low(scores)
    s_last = (scores - s_high.astype(F32) - s_low.astype(F32)).astype(BF16)
    picked = dot_nn(jnp.concatenate([s_high, s_low, s_last], axis=0), pick[...])
    picked = picked[:16] + picked[16:32] + picked[32:]
    part_col = lax.broadcasted_iota(jnp.int32, (16, 128), 1)
    parts[mp] = jnp.where(part_col == 2 * cands, selfterm, picked)
    for step in sorted(range(1, modules), key=lambda step: -min(step, modules - step)):
        pltpu.make_async_remote_copy(
            src_ref=parts.at[mp], dst_ref=parts.at[mp], send_sem=part_send, recv_sem=part_sem.at[mp],
            device_id={"mp": m_peer[step]}, device_id_type=MESH,
        ).start()

    own_tile = feats[:, pl.ds(pl.multiple_of((dp // 2) * 128, 128), 128)].astype(F32).T
    own_rows = jnp.where(dp % 2 == 0, own_tile[:rank], own_tile[rank:]).astype(BF16)
    gram_chunks = 4
    gram_width = gram_ref.shape[1] // gram_chunks
    for chunk in range(gram_chunks):
        cols = slice(chunk * gram_width, (chunk + 1) * gram_width)
        gram_ref[:, cols] = dot_nn(own_rows, feats[:, cols])

    for step in range(1, modules):
        other = m_peer[step]
        pltpu.make_async_remote_copy(
            src_ref=parts.at[other], dst_ref=parts.at[other], send_sem=part_send, recv_sem=part_sem.at[other],
            device_id={"mp": other}, device_id_type=MESH,
        ).wait_recv()
    total = parts[0]
    for m in range(1, modules):
        total = total + parts[m]
    infl_ref[...] = total[:, :2 * cands] / jnp.sqrt(total[:, 2 * cands:2 * cands + 1])

    def all_sent(ref, count, sem):
        pltpu.make_async_remote_copy(
            src_ref=ref.at[pl.ds(0, count)], dst_ref=ref.at[pl.ds(0, count)], send_sem=sem, recv_sem=relay_sem.at[0],
            device_id=mate, device_id_type=MESH,
        ).wait_send()

    own_copies = (NX - 1) + (NZ - 1) + len(NEAR) * (NX - 1)
    wave_copies = sum(len(distances) for distances in WAVES) * (NX - 1)
    all_sent(raw, own_copies + wave_copies, send_sem)
    all_sent(feats, seqs // 2, relay_send)
    all_sent(parts, modules - 1, part_send)


def write_kernel(gram_ref, infl_ref, gram_out, infl_out, gram_sem, infl_sem):
    gram_copy = pltpu.make_async_copy(gram_ref, gram_out, gram_sem)
    infl_copy = pltpu.make_async_copy(infl_ref, infl_out, infl_sem)
    gram_copy.start()
    infl_copy.start()
    infl_copy.wait()
    gram_copy.wait()


def on_device(activations, out_grads, proj_in, proj_out, query_feat, candidates):
    _, seqs, tokens, depth = activations.shape
    rank = proj_in.shape[1]
    queries, size = query_feat.shape[1:]
    modules = lax.axis_size("mp")
    shards = lax.axis_size("dp")
    total = shards * seqs
    vmem = pltpu.VMEM
    dma = pltpu.SemaphoreType.DMA
    gram, influence = pl.pallas_call(
        kernel,
        name="influence",
        out_shape=(
            jax.ShapeDtypeStruct((size // shards, size), F32),
            jax.ShapeDtypeStruct((queries, candidates.shape[1] * seqs), F32),
        ),
        in_specs=[pl.BlockSpec(memory_space=pltpu.HBM)] * 6,
        out_specs=(pl.BlockSpec(memory_space=pltpu.VMEM), pl.BlockSpec(memory_space=pltpu.VMEM)),
        scratch_shapes=[
            pltpu.SMEM(candidates.shape, jnp.int32),
            vmem((seqs * tokens, depth), BF16),
            vmem((seqs * tokens, depth), BF16),
            vmem((rank, depth), BF16),
            vmem((rank, depth), BF16),
            vmem((queries, size), F32),
            vmem((NX * NZ, seqs * size // 128, 128), BF16),
            vmem((total // NC * size // 128, 128), F32),
            vmem((total, size), BF16),
            vmem((rank, seqs * tokens), F32),
            vmem((2 * queries, size), BF16),
            vmem((total, 128), BF16),
            vmem((modules, queries, 128), F32),
            dma((CHUNKS, 4)),
            dma,
            dma,
            dma,
            dma,
            dma((NX, NZ)),
            dma((NX, len(WAVES))),
            dma((NX,)),
            dma,
            dma((modules,)),
        ],
        compiler_params=pltpu.CompilerParams(
            collective_id=0, has_side_effects=True, vmem_limit_bytes=48 * 2**20
        ),
    )(
        *(
            pltpu.with_memory_space_constraint(operand, pltpu.HBM)
            for operand in (
                candidates,
                activations.reshape(seqs * tokens, depth),
                out_grads.reshape(seqs * tokens, depth),
                proj_in.reshape(rank, depth),
                proj_out.reshape(rank, depth),
                query_feat.reshape(queries, size),
            )
        ),
    )
    gram, influence = pl.pallas_call(
        write_kernel,
        name="write",
        out_shape=(jax.ShapeDtypeStruct(gram.shape, F32), jax.ShapeDtypeStruct(influence.shape, F32)),
        in_specs=[pl.BlockSpec(memory_space=pltpu.VMEM)] * 2,
        out_specs=[pl.BlockSpec(memory_space=pltpu.HBM)] * 2,
        scratch_shapes=[dma, dma],
        compiler_params=pltpu.CompilerParams(vmem_limit_bytes=2**20),
    )(gram, influence)
    return gram[None], influence


def solution(mesh):
    placed = (
        P("mp", "dp", None, None),
        P("mp", "dp", None, None),
        P("mp", None, None),
        P("mp", None, None),
        P("mp", "dp", None),
        P("dp", None),
    )
    return jax.shard_map(
        on_device,
        mesh=mesh,
        in_specs=placed,
        out_specs=(P("mp", "dp", None), P("dp", None)),
        check_vma=False,
    )
```
